32 devices in a mesh: store: 8 (over z, x), seq: 4 (over y, core).
Axes of the slice: x: 2, y: 2, z: 4, core: 2. Of those that a mesh axis runs over, the one named last changes fastest.
Arguments:
- activations: bfloat16 [1, 16, 1024, 4096], P(None, 'store', 'seq'), may hold values from -6 to 6
- out_grads: bfloat16 [1, 16, 1024, 4096], P(None, 'store', 'seq'), may hold values from -6 to 6
- proj_in: bfloat16 [1, 64, 4096], replicated, may hold values from -0.09375 to 0.09375
- proj_out: bfloat16 [1, 64, 4096], replicated, may hold values from -0.09375 to 0.09375
- eig_out: float32 [1, 64, 64], replicated, may hold values from -0.75 to 0.75
- eig_in: float32 [1, 64, 64], replicated, may hold values from -0.75 to 0.75
- eig_values: float32 [1, 64, 64], replicated, may hold values from 0.1 to 10
- lengths: int32 [16], P('store'), may hold values from 1 to 1024
- owners: int32 [16], P('store'), may hold values from 0 to 7
- stored: bfloat16 [10240, 4096], P(('store', 'seq')), may hold values from -6 to 6
- queries: bfloat16 [1024, 4096], P('store'), may hold values from -6 to 6
- query_owner: int32 [8], replicated, may hold values from 0 to 7
Outputs:
- stored_scores: float32 [8, 10240, 128], P(None, ('store', 'seq'))
- group_scores: float32 [8, 8, 128], P('store')
The draws below stay inside these ranges and needn't reach their ends.
All inputs are finite; a program needn't handle non-finite values.
Results may differ from the reference program's by a relative error of at most 0.0032.
Values may be sent and summed in bfloat16 or wider, within the bound.
No kernel may reach another device: no remote copies, remote signals or barrier semaphores. Data moves between devices by JAX's collectives and lax.ppermute only.
A program may use at most 128 MiB of HBM per device.

```python
import math
import jax
import jax.numpy as jnp
import numpy as np
from jax import lax

D = 4096
R = 64
L = 1
TS = 256
QP = 128
STEPS = 8
EX = 16
SEQLEN = 1024
FLAT = 4096
STORED = 10240
QUERIES = 1024
N_STORE = 8
N_SEQ = 4


def place_ends(values, stream_key, smallest, largest):
    longest = values.shape.index(max(values.shape))
    spots = []
    for shift in (0, 1):
        where = [jax.random.randint(jax.random.fold_in(stream_key, axis), (), 0, length) for axis, length in enumerate(values.shape)]
        where[longest] = (where[longest] + shift) % values.shape[longest]
        spots.append(tuple(where))
    return values.at[spots[0]].set(smallest).at[spots[1]].set(largest)


def shard_levels(rng, shape, cuts, smallest, largest):
    factor_of, own = 1.0, jax.random.fold_in(rng, 6)
    for axis_at, shards_of in cuts:
        steps = jnp.exp(jax.random.uniform(jax.random.fold_in(own, axis_at), (shards_of,), jnp.float32, smallest / len(cuts), largest / len(cuts)))
        factor_of = factor_of * jnp.repeat(steps, shape[axis_at] // shards_of).reshape([-1 if axis == axis_at else 1 for axis in range(len(shape))])
    return factor_of


def rank_bounds(count, slope):
    weights = [(1 << 20) // math.isqrt(standing ** slope) + 1 for standing in range(1, count + 1)]
    width = 1 + sum(weights) // (1 << 30)
    return np.cumsum(np.array([max(1, weight // width) for weight in weights]))


def ranked(rng, shape, amount, slope):
    grid = rank_bounds(amount, slope)
    pick = jax.random.randint(jax.random.fold_in(rng, 1), shape, 0, int(grid[amount - 1]))
    standing = jnp.searchsorted(jnp.asarray(grid, jnp.int32), pick, side="right")
    return jax.random.permutation(jax.random.fold_in(rng, 2), amount)[standing].astype(jnp.int32)


def normal_values(own_key, extent, width, reach, cuts=(), kind=jnp.bfloat16):
    drawn = jax.random.normal(own_key, extent, jnp.float32) * width
    if len(cuts) > 0:
        drawn = shard_levels(own_key, extent, cuts, -0.22, 0.18) * drawn
    return jnp.clip(drawn, min=-reach, max=reach).astype(kind)


def setup_inputs(seed: int = 0) -> dict:
    seeds = jax.random.split(jax.random.key(seed), 13)
    activations = normal_values(seeds[0], (L, EX, SEQLEN, D), 1.0, 6.0, ((1, 8), (2, 4)))
    out_grads = normal_values(seeds[1], (L, EX, SEQLEN, D), 1.0, 6.0, ((1, 8), (2, 4)))
    proj_in = normal_values(seeds[2], (L, R, D), D ** -0.5, 0.09375)
    proj_out = normal_values(seeds[3], (L, R, D), D ** -0.5, 0.09375)
    eig_out = normal_values(seeds[4], (L, R, R), R ** -0.5, 0.75, (), jnp.float32)
    eig_in = normal_values(seeds[5], (L, R, R), R ** -0.5, 0.75, (), jnp.float32)
    eig_values = jnp.clip(jnp.exp(jax.random.uniform(seeds[6], (L, R, R), jnp.float32, math.log(0.1), math.log(10.0))), 0.1, 10.0)
    lengths = place_ends(jax.random.randint(seeds[7], (EX,), 1, TS * N_SEQ + 1), jax.random.fold_in(seeds[7], 1), 1, TS * N_SEQ).astype(jnp.int32)
    owners = place_ends(ranked(seeds[8], (EX,), N_STORE, 2), jax.random.fold_in(seeds[8], 3), 0, N_STORE - 1).astype(jnp.int32)
    stored = normal_values(seeds[9], (STORED, FLAT), 1.0, 6.0, ((0, 32),))
    queries = normal_values(seeds[10], (QUERIES, FLAT), 1.0, 6.0, ((0, 8),))
    query_owner = place_ends(jax.random.randint(seeds[11], (STEPS,), 0, N_STORE), jax.random.fold_in(seeds[11], 1), 0, N_STORE - 1).astype(jnp.int32)
    return dict(activations=activations, out_grads=out_grads, proj_in=proj_in, proj_out=proj_out, eig_out=eig_out, eig_in=eig_in, eig_values=eig_values, lengths=lengths, owners=owners, stored=stored, queries=queries, query_owner=query_owner)


def precondition(group, eig_out, eig_in, eig_values):
    row_count = group.shape[0]
    layers = eig_out.shape[0]
    rank = eig_out.shape[1]
    blocks = group.reshape(row_count, layers, rank, rank)
    highest = lax.Precision.HIGHEST
    rotated = jnp.einsum('lri,olrs->olis', eig_out, blocks, precision=highest)
    rotated = jnp.einsum('olis,lsj->olij', rotated, eig_in, precision=highest)
    scaled = rotated / eig_values[None]
    restored = jnp.einsum('lri,olij->olrj', eig_out, scaled, precision=highest)
    restored = jnp.einsum('olrj,lsj->olrs', restored, eig_in, precision=highest)
    return restored.reshape(row_count, layers * rank * rank).astype(jnp.bfloat16)

def project_layer(inputs, outgoing, weight_in, weight_out, valid, factor):
    in_side = jnp.einsum('etd,rd->etr', inputs, weight_in, preferred_element_type=jnp.float32)
    out_side = jnp.einsum('etd,rd->etr', outgoing, weight_out, preferred_element_type=jnp.float32)
    weighted = out_side * valid[:, :, None]
    blocks = jnp.einsum('etr,ets->ers', weighted, in_side, precision=lax.Precision.HIGHEST) * factor
    return blocks.reshape(blocks.shape[0], -1)

def reference(activations, out_grads, proj_in, proj_out, eig_out, eig_in, eig_values, lengths, owners, stored, queries, query_owner):
    positions = jnp.arange(SEQLEN, dtype=jnp.int32)
    valid = (positions[None, :] < lengths[:, None]).astype(jnp.float32)
    factor = jnp.float32(1.0 / math.sqrt(SEQLEN))
    partial_value = jnp.concatenate([project_layer(activations[layer], out_grads[layer], proj_in[layer], proj_out[layer], valid, factor) for layer in range(L)], axis=1)
    select = (owners[None, :] == jnp.arange(N_STORE, dtype=jnp.int32)[:, None]).astype(jnp.float32)
    group = jnp.dot(select, partial_value, precision=lax.Precision.HIGHEST)
    precond = precondition(group, eig_out, eig_in, eig_values)
    score_scale = jnp.float32(1.0 / math.sqrt(FLAT))
    stored_list = []
    group_list = []
    for step_index in range(STEPS):
        start = (query_owner[step_index] * QP).astype(jnp.int32)
        panel_rows = lax.dynamic_slice_in_dim(queries, start, QP, 0)
        stored_list.append(lax.dot_general(stored, panel_rows, (((1,), (1,)), ((), ())), preferred_element_type=jnp.float32) * score_scale)
        group_list.append(lax.dot_general(precond, panel_rows, (((1,), (1,)), ((), ())), preferred_element_type=jnp.float32) * score_scale)
    return (jnp.stack(stored_list, axis=0), jnp.stack(group_list, axis=1))
```

```python
import functools
import math

import jax
import jax.numpy as jnp
from jax import lax
from jax.experimental import pallas as pl
from jax.experimental.pallas import tpu as pltpu
from jax.sharding import PartitionSpec as P

AXES = ("store", "seq")
HIGHEST = lax.Precision.HIGHEST
NT = (((1,), (1,)), ((), ()))
MIB = 1 << 20

STEPS = (
    (0, "W", "X", True),
    (1, "Z", "X", False),
    (1, "Y", "Y", False),
    (2, "X", "W", False),
    (4, "Z", "X", False),
    (4, "Y", "Y", False),
    (3, "Z", "X", False),
)
EARLY, MIDDLE, LATE = (1, 2, 3, 4), (5,), (6, 7)


def ring_place(z):
    return z ^ (z >> 1)


def neighbour(way, z, x, y):
    if way == "X":
        return z, 1 - x, y
    if way == "Y":
        return z, x, 1 - y
    if way == "Z":
        return ring_place((ring_place(z) + 1) % 4), x, y
    if way == "W":
        return ring_place((ring_place(z) + 3) % 4), x, y
    if way == "S":
        return z ^ 1, x, y
    if way == "T":
        return z ^ 2, x, y
    return z, x, y


def pairs(way0, way1, swap):
    out = []
    for z in range(4):
        for x in range(2):
            for y in range(2):
                for core in range(2):
                    z2, x2, y2 = neighbour(way1 if core else way0, z, x, y)
                    core2 = 1 - core if swap else core
                    out.append(((z * 2 + x) * 4 + y * 2 + core, (z2 * 2 + x2) * 4 + y2 * 2 + core2))
    return out


def move(array, way0, way1, swap=False):
    return lax.ppermute(array, AXES, pairs(way0, way1, swap))


def contents():
    have = [((0, 0, 0), (0, 0, 1))]
    for source, way0, way1, swap in STEPS:
        got = [None, None]
        for core, way in ((0, way0), (1, way1)):
            ring, across, half = have[source][core]
            if way == "X":
                across = 1 - across
            elif way == "Y":
                half = 1 - half
            elif way == "Z":
                ring = (ring + 1) % 4
            elif way == "W":
                ring = (ring + 3) % 4
            got[1 - core if swap else core] = (ring, across, half)
        have.append(tuple(got))
    return have


CONTENTS = contents()


def unit_place(step, partner, store, seq):
    y, core = seq // 2, seq % 2
    z, x = store // 2, store % 2
    first, second = CONTENTS[step]
    mine = core if not partner else 1 - core
    pick = [jnp.where(mine == 0, a, b) for a, b in zip(first, second, strict=True)]
    place = (ring_place(z) + 4 - pick[0]) % 4
    return ring_place(place) * 2 + (x ^ pick[1]), pick[2] ^ y


def project_kernel(lengths, owners, acts, grads, weight_in, weight_out, out, total, *, factor, owner_count):
    step = pl.program_id(0)
    per = pl.num_programs(0) // lengths.shape[0]
    rows = acts.shape[0]
    example = step // per
    start = lax.axis_index("seq") * (rows * per) + (step % per) * rows
    in_side = lax.dot_general(acts[...], weight_in[...], NT, preferred_element_type=jnp.float32)
    out_side = lax.dot_general(grads[...], weight_out[...], NT, preferred_element_type=jnp.float32)
    positions = start + lax.broadcasted_iota(jnp.int32, out_side.shape, 0)
    out_side = jnp.where(positions < lengths[example], out_side, 0.0)
    block = lax.dot_general(
        out_side, in_side, (((0,), (0,)), ((), ())), precision=HIGHEST, preferred_element_type=jnp.float32
    )

    @pl.when(step % per == 0)
    def _():
        total[example] = block

    @pl.when(step % per != 0)
    def _():
        total[example] += block

    @pl.when(step == pl.num_programs(0) - 1)
    def _():
        for owner in range(owner_count):
            acc = jnp.zeros_like(block)
            for e in range(lengths.shape[0]):
                acc += jnp.where(owners[e] == owner, total[e], 0.0)
            acc = acc * factor
            half = acc.shape[0] // 2
            out[owner] = jnp.concatenate([acc[:half], acc[half:]], axis=1)


def project(acts, grads, weight_in, weight_out, lengths, owners, factor, owner_count):
    examples, tokens, width = acts.shape
    rank = weight_in.shape[0]
    per = 2
    rows = tokens // per
    smem = pl.BlockSpec(memory_space=pltpu.SMEM)
    return pl.pallas_call(
        functools.partial(project_kernel, factor=factor, owner_count=owner_count),
        grid=(examples * per,),
        in_specs=[
            smem,
            smem,
            pl.BlockSpec((rows, width), lambda i: (i, 0)),
            pl.BlockSpec((rows, width), lambda i: (i, 0)),
            pl.BlockSpec((rank, width), lambda i: (0, 0)),
            pl.BlockSpec((rank, width), lambda i: (0, 0)),
        ],
        out_specs=pl.BlockSpec((owner_count, rank // 2, rank * 2), lambda i: (0, 0, 0)),
        out_shape=jax.ShapeDtypeStruct((owner_count, rank // 2, rank * 2), jnp.float32),
        scratch_shapes=[pltpu.VMEM((examples, rank, rank), jnp.float32)],
        compiler_params=pltpu.CompilerParams(vmem_limit_bytes=16 * MIB),
        cost_estimate=pl.CostEstimate(
            flops=4 * examples * tokens * width * rank,
            bytes_accessed=4 * examples * tokens * width,
            transcendentals=0,
        ),
    )(
        lengths,
        owners,
        acts.reshape(examples * tokens, width),
        grads.reshape(examples * tokens, width),
        weight_in,
        weight_out,
    )


def precondition_kernel(group, eig_out, eig_in, eig_values, out):
    rank = eig_out.shape[0]
    packed = group[...]
    block = jnp.concatenate([packed[:, :rank], packed[:, rank:]], axis=0)
    dot = functools.partial(lax.dot_general, precision=HIGHEST, preferred_element_type=jnp.float32)
    basis_out, basis_in = eig_out[...], eig_in[...]
    rotated = dot(basis_out, block, (((0,), (0,)), ((), ())))
    rotated = dot(rotated, basis_in, (((1,), (0,)), ((), ())))
    scaled = rotated / eig_values[...]
    restored = dot(basis_out, scaled, (((1,), (0,)), ((), ())))
    restored = dot(restored, basis_in, NT)
    out[...] = restored.astype(jnp.bfloat16)


def precondition(group, eig_out, eig_in, eig_values):
    rank = eig_out.shape[0]
    return pl.pallas_call(
        precondition_kernel,
        out_shape=jax.ShapeDtypeStruct((rank, rank), jnp.bfloat16),
        compiler_params=pltpu.CompilerParams(vmem_limit_bytes=4 * MIB),
        cost_estimate=pl.CostEstimate(flops=1 << 24, bytes_accessed=1 << 17, transcendentals=0),
    )(group, eig_out, eig_in, eig_values)


def add_units(left, units, steps, totals):
    store, seq = lax.axis_index("store"), lax.axis_index("seq")
    for number, unit in enumerate(units):
        panel, half = unit_place(steps[number // 2], number % 2 == 1, store, seq)
        width = unit.shape[1]
        columns = pl.ds(pl.multiple_of(half * width, width), width)
        totals[panel] += lax.dot_general(left(columns), unit[...], NT, preferred_element_type=jnp.float32)


def early_kernel(*refs):
    stored, own = refs[0], refs[1]
    units, out = refs[2:-1], refs[-1]
    out[...] = jnp.zeros_like(out)
    out[lax.axis_index("store")] = lax.dot_general(
        stored[...], own[...], NT, preferred_element_type=jnp.float32
    )
    add_units(lambda columns: stored[:, columns], units, EARLY, out)


def early_scores(stored, own, units, panels):
    rows, width = stored.shape
    return pl.pallas_call(
        early_kernel,
        out_shape=jax.ShapeDtypeStruct((panels, rows, own.shape[0]), jnp.float32),
        compiler_params=pltpu.CompilerParams(vmem_limit_bytes=24 * MIB),
        cost_estimate=pl.CostEstimate(flops=2 * rows * width * 640, bytes_accessed=8 * MIB, transcendentals=0),
    )(stored, own, *units)


def group_kernel(*refs):
    row, own = refs[0], refs[1]
    units, out = refs[2:-1], refs[-1]
    out[...] = jnp.zeros_like(out)

    def left(columns):
        return jnp.broadcast_to(row[:, columns], (out.shape[1], row[:, columns].shape[1]))

    out[lax.axis_index("store")] = lax.dot_general(
        left(slice(None)), own[...], NT, preferred_element_type=jnp.float32
    )
    add_units(left, units, EARLY + MIDDLE, out)


def group_scores(row, own, units, panels):
    return pl.pallas_call(
        group_kernel,
        out_shape=jax.ShapeDtypeStruct((panels, 16, own.shape[0]), jnp.float32),
        compiler_params=pltpu.CompilerParams(vmem_limit_bytes=16 * MIB),
        cost_estimate=pl.CostEstimate(flops=1 << 28, bytes_accessed=8 * MIB, transcendentals=0),
    )(row, own, *units)


def late_kernel(query_owner, stored, row, early, group, *refs, scale):
    units, (out, group_out, totals, group_totals) = refs[:-4], refs[-4:]
    totals[...] = early[...]
    group_totals[...] = group[...]
    add_units(lambda columns: stored[:, columns], units, MIDDLE + LATE, totals)

    def left(columns):
        return jnp.broadcast_to(row[:, columns], (group.shape[1], row[:, columns].shape[1]))

    add_units(left, units[2 * len(MIDDLE) :], LATE, group_totals)
    for step in range(out.shape[0]):
        owner = query_owner[step]
        out[step] = totals[owner] * scale
        group_out[pl.ds(step, 1)] = group_totals[owner][:1] * scale


def late_scores(query_owner, stored, row, early, group, units, scale):
    vmem = pl.BlockSpec(memory_space=pltpu.VMEM)
    steps = query_owner.shape[0]
    _, rows, panel = early.shape
    return pl.pallas_call(
        functools.partial(late_kernel, scale=scale),
        in_specs=[pl.BlockSpec(memory_space=pltpu.SMEM)] + [vmem] * (4 + len(units)),
        out_shape=(
            jax.ShapeDtypeStruct((steps, rows, panel), jnp.float32),
            jax.ShapeDtypeStruct((steps, panel), jnp.float32),
        ),
        scratch_shapes=[pltpu.VMEM(early.shape, jnp.float32), pltpu.VMEM(group.shape, jnp.float32)],
        compiler_params=pltpu.CompilerParams(vmem_limit_bytes=24 * MIB),
        cost_estimate=pl.CostEstimate(flops=1 << 30, bytes_accessed=8 * MIB, transcendentals=0),
    )(query_owner, stored, row, early, group, *units)


def reduce_groups(partial):
    store, seq = lax.axis_index("store"), lax.axis_index("seq")
    z, x = store // 2, store % 2

    def halve(array, bit, way):
        send = lax.dynamic_index_in_dim(array, 1 - bit, 1, keepdims=False)
        keep = lax.dynamic_index_in_dim(array, bit, 1, keepdims=False)
        return keep + move(send, way, way)

    tail = partial.shape[1:]
    rows = halve(partial.reshape((4, 2) + tail), x, "X")
    rows = halve(rows.reshape((2, 2) + tail), z % 2, "S")
    row = halve(rows.reshape((1, 2) + tail), z // 2, "T")[0]
    row = row + move(row, "Y", "Y")
    return row + move(row, "C", "C", True)


def blocks(
    activations,
    out_grads,
    proj_in,
    proj_out,
    eig_out,
    eig_in,
    eig_values,
    lengths,
    owners,
    stored,
    queries,
    query_owner,
):
    seq = lax.axis_index("seq")
    seq_count, store_count = lax.axis_size("seq"), lax.axis_size("store")
    half = queries.shape[1] // 2
    got = [lax.dynamic_slice_in_dim(queries, ((seq // 2 + seq % 2) % 2) * half, half, 1)]
    partner = [None]
    for source, way0, way1, swap in STEPS:
        block = move(got[source], way0, way1, swap)
        got.append(block)
        partner.append(move(block, "C", "C", True))

    def units(steps):
        return [part[step] for step in steps for part in (got, partner)]

    factor = 1.0 / math.sqrt(activations.shape[2] * seq_count)
    partial = project(
        activations[0], out_grads[0], proj_in[0], proj_out[0], lengths, owners, factor, store_count
    )
    group = reduce_groups(partial)
    precond = precondition(group, eig_out[0], eig_in[0], eig_values[0])
    row = precond.reshape(1, -1)
    scale = 1.0 / math.sqrt(stored.shape[1])
    early = early_scores(stored, queries, units(EARLY), store_count)
    group_early = group_scores(row, queries, units(EARLY + MIDDLE), store_count)
    scores, group_out = late_scores(
        query_owner, stored, row, early, group_early, units(MIDDLE + LATE), scale
    )
    return scores, group_out[None]


def from_root(array, axis, root):
    mine = lax.axis_index(axis) == root
    return lax.psum(jnp.where(mine, array, jnp.zeros_like(array)), axis)


def precondition_rows(group, eig_out, eig_in, eig_values):
    row_count = group.shape[0]
    layers = eig_out.shape[0]
    rank = eig_out.shape[1]
    split = group.reshape(row_count, layers, rank, rank)
    rotated = jnp.einsum("lri,olrs->olis", eig_out, split, precision=HIGHEST)
    rotated = jnp.einsum("olis,lsj->olij", rotated, eig_in, precision=HIGHEST)
    scaled = rotated / eig_values[None]
    restored = jnp.einsum("lri,olij->olrj", eig_out, scaled, precision=HIGHEST)
    restored = jnp.einsum("olrj,lsj->olrs", restored, eig_in, precision=HIGHEST)
    return restored.reshape(row_count, layers * rank * rank).astype(jnp.bfloat16)


def project_layer(inputs, outgoing, weight_in, weight_out, valid, factor):
    in_side = jnp.einsum("etd,rd->etr", inputs, weight_in, preferred_element_type=jnp.float32)
    out_side = jnp.einsum("etd,rd->etr", outgoing, weight_out, preferred_element_type=jnp.float32)
    weighted = out_side * valid[:, :, None]
    outer = jnp.einsum("etr,ets->ers", weighted, in_side, precision=HIGHEST) * factor
    return outer.reshape(outer.shape[0], -1)


def owner_sums(owners, sources, count):
    owner_ids = jnp.arange(count, dtype=jnp.int32)
    select = (owners[None, :] == owner_ids[:, None]).astype(jnp.float32)
    return jnp.dot(select, sources, precision=HIGHEST)


def any_mesh(
    activations,
    out_grads,
    proj_in,
    proj_out,
    eig_out,
    eig_in,
    eig_values,
    lengths,
    owners,
    stored,
    queries,
    query_owner,
):
    seq_count = lax.axis_size("seq")
    seq_index = lax.axis_index("seq")
    local_len = activations.shape[2]
    positions = seq_index * local_len + jnp.arange(local_len, dtype=jnp.int32)
    valid = (positions[None, :] < lengths[:, None]).astype(jnp.float32)
    factor = jnp.float32(1.0 / math.sqrt(local_len * seq_count))
    partial_value = project_layer(activations[0], out_grads[0], proj_in[0], proj_out[0], valid, factor)
    summed = lax.psum(partial_value, "seq")
    owned_row = lax.psum_scatter(
        owner_sums(owners, summed, lax.axis_size("store")), "store", scatter_dimension=0, tiled=True
    )
    precond = precondition_rows(owned_row, eig_out, eig_in, eig_values)
    score_scale = jnp.float32(1.0 / math.sqrt(stored.shape[1]))
    stored_list = []
    group_list = []
    for step_index in range(query_owner.shape[0]):
        panel_rows = from_root(queries, "store", query_owner[step_index])
        stored_list.append(
            lax.dot_general(stored, panel_rows, NT, preferred_element_type=jnp.float32) * score_scale
        )
        group_list.append(
            lax.dot_general(precond, panel_rows, NT, preferred_element_type=jnp.float32) * score_scale
        )
    return (jnp.stack(stored_list, axis=0), jnp.stack(group_list, axis=1))


def solution(mesh):
    fits = mesh.shape["store"] == 8 and mesh.shape["seq"] == 4
    return jax.shard_map(
        blocks if fits else any_mesh,
        mesh=mesh,
        in_specs=(
            P(None, "store", "seq", None),
            P(None, "store", "seq", None),
            P(),
            P(),
            P(),
            P(),
            P(),
            P("store"),
            P("store"),
            P(("store", "seq"), None),
            P("store", None),
            P(),
        ),
        out_specs=(P(None, ("store", "seq"), None), P("store", None, None)),
        check_vma=False,
    )
```

```python
import functools
import math

import jax
import jax.numpy as jnp
from jax import lax
from jax.experimental import pallas as pl
from jax.experimental.pallas import tpu as pltpu
from jax.sharding import PartitionSpec as P

AXES = ("store", "seq")
HIGHEST = lax.Precision.HIGHEST
NT = (((1,), (1,)), ((), ()))
MIB = 1 << 20
FIRST_MIB = 20

STEPS = (
    (0, "W", "X", True),
    (1, "Z", "X", False),
    (1, "Y", "Y", False),
    (2, "X", "W", False),
    (4, "Z", "X", False),
    (4, "Y", "Y", False),
    (3, "Z", "X", False),
)

FIRST = (((1, False), None), ((1, True), None))
SECOND = (((2, False), (4, False)), ((2, True), (4, True)))
THIRD = (((3, False), (5, True)), ((3, True), (5, False)))
LAST = (((6, False), (7, False)), ((6, True), (7, True)))


def ring_place(z):
    return z ^ (z >> 1)


def neighbour(way, z, x, y):
    if way == "X":
        return z, 1 - x, y
    if way == "Y":
        return z, x, 1 - y
    if way == "Z":
        return ring_place((ring_place(z) + 1) % 4), x, y
    if way == "W":
        return ring_place((ring_place(z) + 3) % 4), x, y
    if way == "S":
        return z ^ 1, x, y
    if way == "T":
        return z ^ 2, x, y
    if way == "V":
        return z ^ 3, x, y
    if way == "XY":
        return z, 1 - x, 1 - y
    return z, x, y
EARLY = FIRST + SECOND


def pairs(way0, way1, swap):
    out = []
    for z in range(4):
        for x in range(2):
            for y in range(2):
                for core in range(2):
                    z2, x2, y2 = neighbour(way1 if core else way0, z, x, y)
                    core2 = 1 - core if swap else core
                    out.append(((z * 2 + x) * 4 + y * 2 + core, (z2 * 2 + x2) * 4 + y2 * 2 + core2))
    return out


def move(array, way0, way1, swap=False):
    return lax.ppermute(array, AXES, pairs(way0, way1, swap))


def contents():
    have = [((0, 0, 0), (0, 0, 1))]
    for source, way0, way1, swap in STEPS:
        got = [None, None]
        for core, way in ((0, way0), (1, way1)):
            ring, across, half = have[source][core]
            if way == "X":
                across = 1 - across
            elif way == "Y":
                half = 1 - half
            elif way == "Z":
                ring = (ring + 1) % 4
            elif way == "W":
                ring = (ring + 3) % 4
            got[1 - core if swap else core] = (ring, across, half)
        have.append(tuple(got))
    return have


CONTENTS = contents()


def check_pairs():
    seen = [(0, 0, 0), (0, 0, 1)]
    for first, second in FIRST + SECOND + THIRD + LAST:
        for core in range(2):
            one = CONTENTS[first[0]][core ^ first[1]]
            seen.append(one)
            if second is not None:
                two = CONTENTS[second[0]][core ^ second[1]]
                seen.append(two)
                assert one[2] == two[2]
    assert len(set(seen)) == 16


check_pairs()


def unit_place(step, partner, store, seq):
    y, core = seq // 2, seq % 2
    z, x = store // 2, store % 2
    first, second = CONTENTS[step]
    mine = core if not partner else 1 - core
    pick = [jnp.where(mine == 0, a, b) for a, b in zip(first, second, strict=True)]
    place = (ring_place(z) + 4 - pick[0]) % 4
    return ring_place(place) * 2 + (x ^ pick[1]), pick[2] ^ y


def outer_kernel(lengths, owners, in_side, out_side, out, *, factor):
    examples, _, tokens = in_side.shape
    start = lax.axis_index("seq") * tokens
    sums = []
    for e in range(examples):
        outgoing = out_side[e]
        positions = start + lax.broadcasted_iota(jnp.int32, outgoing.shape, 1)
        outgoing = jnp.where(positions < lengths[e], outgoing, 0.0)
        block = lax.dot_general(outgoing, in_side[e], NT, precision=HIGHEST, preferred_element_type=jnp.float32)
        half = block.shape[0] // 2
        sums.append(jnp.concatenate([block[:half], block[half:]], axis=1) * factor)
    for owner in range(out.shape[0]):
        acc = jnp.zeros_like(sums[0])
        for e in range(examples):
            acc += jnp.where(owners[e] == owner, sums[e], 0.0)
        out[owner] = acc


def project(acts, grads, weight_in, weight_out, lengths, owners, factor, owner_count):
    in_side = jnp.einsum("rd,etd->ert", weight_in, acts, preferred_element_type=jnp.float32)
    out_side = jnp.einsum("rd,etd->ert", weight_out, grads, preferred_element_type=jnp.float32)
    rank = weight_in.shape[0]
    smem, vmem = pl.BlockSpec(memory_space=pltpu.SMEM), pl.BlockSpec(memory_space=pltpu.VMEM)
    return pl.pallas_call(
        functools.partial(outer_kernel, factor=factor),
        in_specs=[smem, smem, vmem, vmem],
        out_specs=vmem,
        out_shape=jax.ShapeDtypeStruct((owner_count, rank // 2, rank * 2), jnp.float32),
        compiler_params=pltpu.CompilerParams(vmem_limit_bytes=4 * MIB),
        cost_estimate=pl.CostEstimate(flops=1 << 26, bytes_accessed=1 << 19, transcendentals=0),
    )(lengths, owners, in_side, out_side)


def precondition_kernel(group, eig_out, eig_in, eig_values, out):
    rank = eig_out.shape[0]
    packed = group[...]
    block = jnp.concatenate([packed[:, :rank], packed[:, rank:]], axis=0)
    dot = functools.partial(lax.dot_general, precision=HIGHEST, preferred_element_type=jnp.float32)
    basis_out, basis_in = eig_out[...], eig_in[...]
    rotated = dot(basis_out, block, (((0,), (0,)), ((), ())))
    rotated = dot(rotated, basis_in, (((1,), (0,)), ((), ())))
    scaled = rotated / eig_values[...]
    restored = dot(basis_out, scaled, (((1,), (0,)), ((), ())))
    restored = dot(restored, basis_in, NT)
    out[...] = restored.astype(jnp.bfloat16)


def precondition(group, eig_out, eig_in, eig_values):
    rank = eig_out.shape[0]
    return pl.pallas_call(
        precondition_kernel,
        out_shape=jax.ShapeDtypeStruct((rank, rank), jnp.bfloat16),
        compiler_params=pltpu.CompilerParams(vmem_limit_bytes=4 * MIB),
        cost_estimate=pl.CostEstimate(flops=1 << 24, bytes_accessed=1 << 17, transcendentals=0),
    )(group, eig_out, eig_in, eig_values)


def add_scores(left, own, blocks, names, totals, scale):
    store, seq = lax.axis_index("store"), lax.axis_index("seq")
    for first, second in names:
        panel, half = unit_place(*first, store, seq)
        block = next(blocks)
        rows, width = block.shape
        columns = pl.ds(pl.multiple_of(half * width, width), width)
        if second is None:
            other_panel, other = store, own[:, columns]
        else:
            other_panel, other = unit_place(*second, store, seq)[0], next(blocks)
        product = lax.dot_general(
            left[:, columns], jnp.concatenate([block, other], axis=0), NT, preferred_element_type=jnp.float32
        )
        totals[panel] += product[:, :rows] * scale
        totals[other_panel] += product[:, rows:] * scale


def brought(units, buffer, sems):
    copies = [pltpu.make_async_copy(unit, buffer.at[n], sems.at[n]) for n, unit in enumerate(units)]
    for copy in copies:
        copy.start()

    def each():
        for n, copy in enumerate(copies):
            copy.wait()
            yield buffer[n]

    return each()


def first_kernel(stored, row, own, *refs, names, scale):
    units, (left, totals, token, buffer, sems, own_buffer, own_sems) = refs[:-7], refs[-7:]
    rows = stored.shape[0]
    copies = (
        pltpu.make_async_copy(stored, left.at[pl.ds(0, rows)], own_sems.at[0]),
        pltpu.make_async_copy(own, own_buffer, own_sems.at[1]),
    )
    for copy in copies:
        copy.start()
    blocks = brought(units, buffer, sems)
    token[...] = jnp.zeros_like(token)
    left[rows:] = jnp.broadcast_to(row[...], (left.shape[0] - rows, row.shape[1]))
    totals[...] = jnp.zeros_like(totals)
    for copy in copies:
        copy.wait()
    add_scores(left, own_buffer, blocks, names, totals, scale)


def first_scores(stored, row, own, units, names, scale, panels):
    vmem, anywhere = pl.BlockSpec(memory_space=pltpu.VMEM), pl.BlockSpec(memory_space=pl.ANY)
    rows, width = stored.shape
    panel = own.shape[0]
    return pl.pallas_call(
        functools.partial(first_kernel, names=names, scale=scale),
        in_specs=[anywhere, vmem, anywhere] + [anywhere] * len(units),
        out_specs=(vmem, vmem, vmem),
        out_shape=(
            jax.ShapeDtypeStruct((rows + 16, width), jnp.bfloat16),
            jax.ShapeDtypeStruct((panels, rows + 16, panel), jnp.float32),
            jax.ShapeDtypeStruct((8, 128), jnp.float32),
        ),
        scratch_shapes=[
            pltpu.VMEM((len(units),) + units[0].shape, jnp.bfloat16),
            pltpu.SemaphoreType.DMA((len(units),)),
            pltpu.VMEM(own.shape, jnp.bfloat16),
            pltpu.SemaphoreType.DMA((2,)),
        ],
        compiler_params=pltpu.CompilerParams(vmem_limit_bytes=FIRST_MIB * MIB),
        cost_estimate=pl.CostEstimate(flops=1 << 31, bytes_accessed=4 * MIB, transcendentals=0),
    )(stored, row, own, *units)


def next_kernel(left, before, *refs, names, scale):
    units, (totals, buffer, sems) = refs[:-3], refs[-3:]
    blocks = brought(units, buffer, sems)
    totals[...] = before[...]
    add_scores(left, None, blocks, names, totals, scale)


def next_scores(left, before, units, names, scale):
    vmem, anywhere = pl.BlockSpec(memory_space=pltpu.VMEM), pl.BlockSpec(memory_space=pl.ANY)
    return pl.pallas_call(
        functools.partial(next_kernel, names=names, scale=scale),
        in_specs=[vmem, vmem] + [anywhere] * len(units),
        out_specs=vmem,
        out_shape=jax.ShapeDtypeStruct(before.shape, jnp.float32),
        scratch_shapes=[
            pltpu.VMEM((len(units),) + units[0].shape, jnp.bfloat16),
            pltpu.SemaphoreType.DMA((len(units),)),
        ],
        compiler_params=pltpu.CompilerParams(vmem_limit_bytes=8 * MIB),
        cost_estimate=pl.CostEstimate(flops=1 << 30, bytes_accessed=2 * MIB, transcendentals=0),
    )(left, before, *units)


def last_kernel(query_owner, left, before, *refs, names, scale):
    units, (out, group_out, totals, sems) = refs[:-4], refs[-4:]
    rows = out.shape[1]
    totals[...] = before[...]
    add_scores(left, None, iter([unit[...] for unit in units]), names, totals, scale)
    copies = []
    for step in range(out.shape[0]):
        owner = query_owner[step]
        copies.append(pltpu.make_async_copy(totals.at[owner, pl.ds(0, rows)], out.at[step], sems.at[step]))
        copies[-1].start()
        group_out[pl.ds(step, 1)] = totals[owner, rows : rows + 1]
    for copy in copies:
        copy.wait()


def last_scores(query_owner, left, before, units, names, scale):
    vmem, anywhere = pl.BlockSpec(memory_space=pltpu.VMEM), pl.BlockSpec(memory_space=pl.ANY)
    steps = query_owner.shape[0]
    _, rows, panel = before.shape
    return pl.pallas_call(
        functools.partial(last_kernel, names=names, scale=scale),
        in_specs=[pl.BlockSpec(memory_space=pltpu.SMEM)] + [vmem] * (2 + len(units)),
        out_specs=(anywhere, vmem),
        out_shape=(
            jax.ShapeDtypeStruct((steps, rows - 16, panel), jnp.float32),
            jax.ShapeDtypeStruct((steps, panel), jnp.float32),
        ),
        scratch_shapes=[pltpu.VMEM(before.shape, jnp.float32), pltpu.SemaphoreType.DMA((steps,))],
        compiler_params=pltpu.CompilerParams(vmem_limit_bytes=8 * MIB),
        cost_estimate=pl.CostEstimate(flops=1 << 30, bytes_accessed=8 * MIB, transcendentals=0),
    )(query_owner, left, before, *units)


def gate_kernel(block, *refs):
    del block, refs


def gate(block, *others):
    vmem, anywhere = pl.BlockSpec(memory_space=pltpu.VMEM), pl.BlockSpec(memory_space=pl.ANY)
    return pl.pallas_call(
        gate_kernel,
        in_specs=[anywhere] + [vmem if other.dtype == jnp.float32 else anywhere for other in others],
        out_specs=anywhere,
        out_shape=jax.ShapeDtypeStruct(block.shape, block.dtype),
        input_output_aliases={0: 0},
        compiler_params=pltpu.CompilerParams(vmem_limit_bytes=MIB),
        cost_estimate=pl.CostEstimate(flops=0, bytes_accessed=0, transcendentals=0),
    )(block, *others)


def plane_kernel(rows, sent, *refs):
    received, (kept, *sends) = refs[:3], refs[-4:]
    del sent
    store = lax.axis_index("store")
    z, x = store // 2, store % 2
    for place in range(rows.shape[0] // 2):
        kept[place] = rows[2 * place + x] + received[0][place] + received[1][place] + received[2][place]
    for bits, send in enumerate(sends):
        send[0] = kept[z ^ (bits + 1)]


def sum_plane(rows, others, *tokens):
    vmem, anywhere = pl.BlockSpec(memory_space=pltpu.VMEM), pl.BlockSpec(memory_space=pl.ANY)
    keep, send = others
    came = (move(send, "X", "X"), move(keep, "Y", "Y"), move(send, "XY", "XY"))
    count, tail = keep.shape[0], keep.shape[1:]
    return pl.pallas_call(
        plane_kernel,
        in_specs=[vmem] * 5 + [anywhere] * len(tokens),
        out_specs=[vmem] * 4,
        out_shape=[jax.ShapeDtypeStruct((count,) + tail, jnp.float32)]
        + [jax.ShapeDtypeStruct((1,) + tail, jnp.float32)] * 3,
        compiler_params=pltpu.CompilerParams(vmem_limit_bytes=4 * MIB),
        cost_estimate=pl.CostEstimate(flops=1 << 16, bytes_accessed=1 << 18, transcendentals=0),
    )(rows, send, *came, *tokens)


def line_kernel(rows, *refs):
    out = refs[-1]
    out[...] = rows[lax.axis_index("store") // 2] + refs[0][0] + refs[1][0] + refs[2][0]


def sum_line(rows, sends, *tokens):
    vmem, anywhere = pl.BlockSpec(memory_space=pltpu.VMEM), pl.BlockSpec(memory_space=pl.ANY)
    came = [move(send, way, way) for way, send in zip("STV", sends, strict=True)]
    return pl.pallas_call(
        line_kernel,
        in_specs=[vmem] * 4 + [anywhere] * len(tokens),
        out_specs=vmem,
        out_shape=jax.ShapeDtypeStruct(rows.shape[1:], jnp.float32),
        compiler_params=pltpu.CompilerParams(vmem_limit_bytes=4 * MIB),
        cost_estimate=pl.CostEstimate(flops=1 << 16, bytes_accessed=1 << 18, transcendentals=0),
    )(rows, *came, *tokens)


def split_kernel(rows, other, total, keep, send):
    x = lax.axis_index("store") % 2
    total[...] = rows[...] + other[...]
    for place in range(keep.shape[0]):
        keep[place] = total[2 * place + x]
        send[place] = total[2 * place + 1 - x]


def sum_cores(rows):
    vmem = pl.BlockSpec(memory_space=pltpu.VMEM)
    count, tail = rows.shape[0], rows.shape[1:]
    part = jax.ShapeDtypeStruct((count // 2,) + tail, jnp.float32)
    return pl.pallas_call(
        split_kernel,
        in_specs=[vmem] * 2,
        out_specs=[vmem] * 3,
        out_shape=[jax.ShapeDtypeStruct(rows.shape, jnp.float32), part, part],
        compiler_params=pltpu.CompilerParams(vmem_limit_bytes=4 * MIB),
        cost_estimate=pl.CostEstimate(flops=1 << 16, bytes_accessed=1 << 18, transcendentals=0),
    )(rows, move(rows, "C", "C", True))


def blocks(
    activations,
    out_grads,
    proj_in,
    proj_out,
    eig_out,
    eig_in,
    eig_values,
    lengths,
    owners,
    stored,
    queries,
    query_owner,
):
    seq = lax.axis_index("seq")
    seq_count, store_count = lax.axis_size("seq"), lax.axis_size("store")
    half = queries.shape[1] // 2
    got = {0: lax.dynamic_slice_in_dim(queries, ((seq // 2 + seq % 2) % 2) * half, half, 1)}
    partner = {}
    scale = 1.0 / math.sqrt(stored.shape[1])
    factor = 1.0 / math.sqrt(activations.shape[2] * seq_count)

    def step(number, part=None):
        source, way0, way1, swap = STEPS[number - 1]
        if part is None:
            got[number] = move(got[source], way0, way1, swap)
        else:
            width = half // 2
            got[number, part] = move(got[source][:, part * width : (part + 1) * width], way0, way1, swap)

    def swap(*numbers):
        for number in numbers:
            partner[number] = move(got[number], "C", "C", True)

    def pick(names):
        return [(partner if name[1] else got)[name[0]] for pair in names for name in pair if name is not None]

    def after(number, *others):
        got[number] = gate(got[number], *others)

    step(1)
    partial = project(
        activations[0], out_grads[0], proj_in[0], proj_out[0], lengths, owners, factor, store_count
    )
    after(1, partial)
    step(2)
    step(3, 0)
    swap(1)
    rows, *others = sum_cores(partial)
    rows, *others = sum_plane(rows, others, got[2])
    after(2, got[3, 0])
    step(4)
    step(3, 1)
    swap(2)
    row = sum_line(rows, others, got[4])
    after(4, got[3, 1])
    step(5)
    step(6, 0)
    swap(4)
    precond = precondition(row, eig_out[0], eig_in[0], eig_values[0]).reshape(1, -1)
    left, total, token = first_scores(stored, precond, queries, pick(EARLY), EARLY, scale, store_count)
    got[3] = jnp.concatenate([got[3, 0], got[3, 1]], axis=1)
    after(3, token, got[6, 0])
    step(7)
    step(6, 1)
    swap(3, 5)
    total = next_scores(left, total, pick(THIRD), THIRD, scale)
    got[6] = jnp.concatenate([got[6, 0], got[6, 1]], axis=1)
    swap(6, 7)
    scores, group_out = last_scores(query_owner, left, total, pick(LAST), LAST, scale)
    return scores, group_out[None]


def from_root(array, axis, root):
    mine = lax.axis_index(axis) == root
    return lax.psum(jnp.where(mine, array, jnp.zeros_like(array)), axis)


def precondition_rows(group, eig_out, eig_in, eig_values):
    row_count = group.shape[0]
    layers = eig_out.shape[0]
    rank = eig_out.shape[1]
    split = group.reshape(row_count, layers, rank, rank)
    rotated = jnp.einsum("lri,olrs->olis", eig_out, split, precision=HIGHEST)
    rotated = jnp.einsum("olis,lsj->olij", rotated, eig_in, precision=HIGHEST)
    scaled = rotated / eig_values[None]
    restored = jnp.einsum("lri,olij->olrj", eig_out, scaled, precision=HIGHEST)
    restored = jnp.einsum("olrj,lsj->olrs", restored, eig_in, precision=HIGHEST)
    return restored.reshape(row_count, layers * rank * rank).astype(jnp.bfloat16)


def project_layer(inputs, outgoing, weight_in, weight_out, valid, factor):
    in_side = jnp.einsum("etd,rd->etr", inputs, weight_in, preferred_element_type=jnp.float32)
    out_side = jnp.einsum("etd,rd->etr", outgoing, weight_out, preferred_element_type=jnp.float32)
    weighted = out_side * valid[:, :, None]
    outer = jnp.einsum("etr,ets->ers", weighted, in_side, precision=HIGHEST) * factor
    return outer.reshape(outer.shape[0], -1)


def owner_sums(owners, sources, count):
    owner_ids = jnp.arange(count, dtype=jnp.int32)
    select = (owners[None, :] == owner_ids[:, None]).astype(jnp.float32)
    return jnp.dot(select, sources, precision=HIGHEST)


def any_mesh(
    activations,
    out_grads,
    proj_in,
    proj_out,
    eig_out,
    eig_in,
    eig_values,
    lengths,
    owners,
    stored,
    queries,
    query_owner,
):
    seq_count = lax.axis_size("seq")
    seq_index = lax.axis_index("seq")
    local_len = activations.shape[2]
    positions = seq_index * local_len + jnp.arange(local_len, dtype=jnp.int32)
    valid = (positions[None, :] < lengths[:, None]).astype(jnp.float32)
    factor = jnp.float32(1.0 / math.sqrt(local_len * seq_count))
    partial_value = project_layer(activations[0], out_grads[0], proj_in[0], proj_out[0], valid, factor)
    summed = lax.psum(partial_value, "seq")
    owned_row = lax.psum_scatter(
        owner_sums(owners, summed, lax.axis_size("store")), "store", scatter_dimension=0, tiled=True
    )
    precond = precondition_rows(owned_row, eig_out, eig_in, eig_values)
    score_scale = jnp.float32(1.0 / math.sqrt(stored.shape[1]))
    stored_list = []
    group_list = []
    for step_index in range(query_owner.shape[0]):
        panel_rows = from_root(queries, "store", query_owner[step_index])
        stored_list.append(
            lax.dot_general(stored, panel_rows, NT, preferred_element_type=jnp.float32) * score_scale
        )
        group_list.append(
            lax.dot_general(precond, panel_rows, NT, preferred_element_type=jnp.float32) * score_scale
        )
    return (jnp.stack(stored_list, axis=0), jnp.stack(group_list, axis=1))


def solution(mesh):
    fits = mesh.shape["store"] == 8 and mesh.shape["seq"] == 4
    return jax.shard_map(
        blocks if fits else any_mesh,
        mesh=mesh,
        in_specs=(
            P(None, "store", "seq", None),
            P(None, "store", "seq", None),
            P(),
            P(),
            P(),
            P(),
            P(),
            P("store"),
            P("store"),
            P(("store", "seq"), None),
            P("store", None),
            P(),
        ),
        out_specs=(P(None, ("store", "seq"), None), P("store", None, None)),
        check_vma=False,
    )
```

```python
import functools
import math

import jax
import jax.numpy as jnp
from jax import lax
from jax.experimental import pallas as pl
from jax.experimental.pallas import tpu as pltpu
from jax.sharding import PartitionSpec as P

AXES = ("store", "seq")
HIGHEST = lax.Precision.HIGHEST
NT = (((1,), (1,)), ((), ()))
MIB = 1 << 20

STEPS = (
    (0, "W", "X", True),
    (1, "Z", "X", False),
    (1, "Y", "Y", False),
    (2, "X", "W", False),
    (4, "Z", "X", False),
    (4, "Y", "Y", False),
    (3, "Z", "X", False),
)

FIRST = (((1, False), None), ((1, True), None))
SECOND = (((2, False), (4, False)), ((2, True), (4, True)))
THIRD = (((3, False), (5, True)), ((3, True), (5, False)))
LAST = (((6, False), (7, False)), ((6, True), (7, True)))


def ring_place(z):
    return z ^ (z >> 1)


def neighbour(way, z, x, y):
    if way == "X":
        return z, 1 - x, y
    if way == "Y":
        return z, x, 1 - y
    if way == "Z":
        return ring_place((ring_place(z) + 1) % 4), x, y
    if way == "W":
        return ring_place((ring_place(z) + 3) % 4), x, y
    if way == "S":
        return z ^ 1, x, y
    if way == "T":
        return z ^ 2, x, y
    if way == "V":
        return z ^ 3, x, y
    if way == "XY":
        return z, 1 - x, 1 - y
    return z, x, y
EARLY = FIRST + SECOND


def pairs(way0, way1, swap):
    out = []
    for z in range(4):
        for x in range(2):
            for y in range(2):
                for core in range(2):
                    z2, x2, y2 = neighbour(way1 if core else way0, z, x, y)
                    core2 = 1 - core if swap else core
                    out.append(((z * 2 + x) * 4 + y * 2 + core, (z2 * 2 + x2) * 4 + y2 * 2 + core2))
    return out


def move(array, way0, way1, swap=False):
    return lax.ppermute(array, AXES, pairs(way0, way1, swap))


def contents():
    have = [((0, 0, 0), (0, 0, 1))]
    for source, way0, way1, swap in STEPS:
        got = [None, None]
        for core, way in ((0, way0), (1, way1)):
            ring, across, half = have[source][core]
            if way == "X":
                across = 1 - across
            elif way == "Y":
                half = 1 - half
            elif way == "Z":
                ring = (ring + 1) % 4
            elif way == "W":
                ring = (ring + 3) % 4
            got[1 - core if swap else core] = (ring, across, half)
        have.append(tuple(got))
    return have


CONTENTS = contents()


def check_pairs():
    seen = [(0, 0, 0), (0, 0, 1)]
    for first, second in FIRST + SECOND + THIRD + LAST:
        for core in range(2):
            one = CONTENTS[first[0]][core ^ first[1]]
            seen.append(one)
            if second is not None:
                two = CONTENTS[second[0]][core ^ second[1]]
                seen.append(two)
                assert one[2] == two[2]
    assert len(set(seen)) == 16


check_pairs()


def unit_place(step, partner, store, seq):
    y, core = seq // 2, seq % 2
    z, x = store // 2, store % 2
    first, second = CONTENTS[step]
    mine = core if not partner else 1 - core
    pick = [jnp.where(mine == 0, a, b) for a, b in zip(first, second, strict=True)]
    place = (ring_place(z) + 4 - pick[0]) % 4
    return ring_place(place) * 2 + (x ^ pick[1]), pick[2] ^ y


def outer_kernel(lengths, owners, in_side, out_side, out, *, factor):
    examples, _, tokens = in_side.shape
    start = lax.axis_index("seq") * tokens
    sums = []
    for e in range(examples):
        outgoing = out_side[e]
        positions = start + lax.broadcasted_iota(jnp.int32, outgoing.shape, 1)
        outgoing = jnp.where(positions < lengths[e], outgoing, 0.0)
        block = lax.dot_general(outgoing, in_side[e], NT, precision=HIGHEST, preferred_element_type=jnp.float32)
        half = block.shape[0] // 2
        sums.append(jnp.concatenate([block[:half], block[half:]], axis=1) * factor)
    for owner in range(out.shape[0]):
        acc = jnp.zeros_like(sums[0])
        for e in range(examples):
            acc += jnp.where(owners[e] == owner, sums[e], 0.0)
        out[owner] = acc


def project(acts, grads, weight_in, weight_out, lengths, owners, factor, owner_count):
    in_side = jnp.einsum("rd,etd->ert", weight_in, acts, preferred_element_type=jnp.float32)
    out_side = jnp.einsum("rd,etd->ert", weight_out, grads, preferred_element_type=jnp.float32)
    rank = weight_in.shape[0]
    smem, vmem = pl.BlockSpec(memory_space=pltpu.SMEM), pl.BlockSpec(memory_space=pltpu.VMEM)
    return pl.pallas_call(
        functools.partial(outer_kernel, factor=factor),
        in_specs=[smem, smem, vmem, vmem],
        out_specs=vmem,
        out_shape=jax.ShapeDtypeStruct((owner_count, rank // 2, rank * 2), jnp.float32),
        compiler_params=pltpu.CompilerParams(vmem_limit_bytes=4 * MIB),
        cost_estimate=pl.CostEstimate(flops=1 << 26, bytes_accessed=1 << 19, transcendentals=0),
    )(lengths, owners, in_side, out_side)


def precondition_kernel(group, eig_out, eig_in, eig_values, out):
    rank = eig_out.shape[0]
    packed = group[...]
    block = jnp.concatenate([packed[:, :rank], packed[:, rank:]], axis=0)
    dot = functools.partial(lax.dot_general, precision=HIGHEST, preferred_element_type=jnp.float32)
    basis_out, basis_in = eig_out[...], eig_in[...]
    rotated = dot(basis_out, block, (((0,), (0,)), ((), ())))
    rotated = dot(rotated, basis_in, (((1,), (0,)), ((), ())))
    scaled = rotated / eig_values[...]
    restored = dot(basis_out, scaled, (((1,), (0,)), ((), ())))
    restored = dot(restored, basis_in, NT)
    out[...] = restored.astype(jnp.bfloat16)


def precondition(group, eig_out, eig_in, eig_values):
    rank = eig_out.shape[0]
    return pl.pallas_call(
        precondition_kernel,
        out_shape=jax.ShapeDtypeStruct((rank, rank), jnp.bfloat16),
        compiler_params=pltpu.CompilerParams(vmem_limit_bytes=4 * MIB),
        cost_estimate=pl.CostEstimate(flops=1 << 24, bytes_accessed=1 << 17, transcendentals=0),
    )(group, eig_out, eig_in, eig_values)


def add_scores(left, own, blocks, names, totals, scale):
    store, seq = lax.axis_index("store"), lax.axis_index("seq")
    for first, second in names:
        panel, half = unit_place(*first, store, seq)
        block = next(blocks)
        rows, width = block.shape
        columns = pl.ds(pl.multiple_of(half * width, width), width)
        if second is None:
            other_panel, other = store, own[:, columns]
        else:
            other_panel, other = unit_place(*second, store, seq)[0], next(blocks)
        product = lax.dot_general(
            left[:, columns], jnp.concatenate([block, other], axis=0), NT, preferred_element_type=jnp.float32
        )
        totals[panel] += product[:, :rows] * scale
        totals[other_panel] += product[:, rows:] * scale


def brought(units, buffer, sems):
    copies = [pltpu.make_async_copy(unit, buffer.at[n], sems.at[n]) for n, unit in enumerate(units)]
    for copy in copies:
        copy.start()

    def each():
        for n, copy in enumerate(copies):
            copy.wait()
            yield buffer[n]

    return each()


def first_kernel(stored, row, own, *refs, names, scale):
    units, (left, totals, token, buffer, sems, own_buffer, own_sems) = refs[:-7], refs[-7:]
    rows = stored.shape[0]
    copies = (
        pltpu.make_async_copy(stored, left.at[pl.ds(0, rows)], own_sems.at[0]),
        pltpu.make_async_copy(own, own_buffer, own_sems.at[1]),
    )
    for copy in copies:
        copy.start()
    blocks = brought(units, buffer, sems)
    token[...] = jnp.zeros_like(token)
    left[rows:] = jnp.broadcast_to(row[...], (left.shape[0] - rows, row.shape[1]))
    totals[...] = jnp.zeros_like(totals)
    for copy in copies:
        copy.wait()
    add_scores(left, own_buffer, blocks, names, totals, scale)


def first_scores(stored, row, own, units, names, scale, panels):
    vmem, anywhere = pl.BlockSpec(memory_space=pltpu.VMEM), pl.BlockSpec(memory_space=pl.ANY)
    rows, width = stored.shape
    panel = own.shape[0]
    return pl.pallas_call(
        functools.partial(first_kernel, names=names, scale=scale),
        in_specs=[anywhere, vmem, anywhere] + [anywhere] * len(units),
        out_specs=(vmem, vmem, vmem),
        out_shape=(
            jax.ShapeDtypeStruct((rows + 16, width), jnp.bfloat16),
            jax.ShapeDtypeStruct((panels, rows + 16, panel), jnp.float32),
            jax.ShapeDtypeStruct((8, 128), jnp.float32),
        ),
        scratch_shapes=[
            pltpu.VMEM((len(units),) + units[0].shape, jnp.bfloat16),
            pltpu.SemaphoreType.DMA((len(units),)),
            pltpu.VMEM(own.shape, jnp.bfloat16),
            pltpu.SemaphoreType.DMA((2,)),
        ],
        compiler_params=pltpu.CompilerParams(vmem_limit_bytes=20 * MIB),
        cost_estimate=pl.CostEstimate(flops=1 << 33, bytes_accessed=1024, transcendentals=0),
    )(stored, row, own, *units)


def next_kernel(left, before, *refs, names, scale):
    units, (totals, buffer, sems) = refs[:-3], refs[-3:]
    blocks = brought(units, buffer, sems)
    totals[...] = before[...]
    add_scores(left, None, blocks, names, totals, scale)


def next_scores(left, before, units, names, scale):
    vmem, anywhere = pl.BlockSpec(memory_space=pltpu.VMEM), pl.BlockSpec(memory_space=pl.ANY)
    return pl.pallas_call(
        functools.partial(next_kernel, names=names, scale=scale),
        in_specs=[vmem, vmem] + [anywhere] * len(units),
        out_specs=vmem,
        out_shape=jax.ShapeDtypeStruct(before.shape, jnp.float32),
        scratch_shapes=[
            pltpu.VMEM((len(units),) + units[0].shape, jnp.bfloat16),
            pltpu.SemaphoreType.DMA((len(units),)),
        ],
        compiler_params=pltpu.CompilerParams(vmem_limit_bytes=8 * MIB),
        cost_estimate=pl.CostEstimate(flops=1 << 32, bytes_accessed=1024, transcendentals=0),
    )(left, before, *units)


def last_kernel(query_owner, left, before, *refs, names, scale):
    units, (out, group_out, totals, sems) = refs[:-4], refs[-4:]
    rows = out.shape[1]
    store, seq = lax.axis_index("store"), lax.axis_index("seq")
    late = [unit_place(*name, store, seq)[0] for pair in names for name in pair]

    def copy_out(source, step):
        return pltpu.make_async_copy(source.at[query_owner[step], pl.ds(0, rows)], out.at[step], sems.at[step])

    def is_late(step):
        found = query_owner[step] == late[0]
        for panel in late[1:]:
            found = found | (query_owner[step] == panel)
        return found

    for step in range(out.shape[0]):

        @pl.when(jnp.logical_not(is_late(step)))
        def _(step=step):
            copy_out(before, step).start()

    totals[...] = before[...]
    add_scores(left, None, iter([unit[...] for unit in units]), names, totals, scale)
    for step in range(out.shape[0]):

        @pl.when(is_late(step))
        def _(step=step):
            copy_out(totals, step).start()

        group_out[pl.ds(step, 1)] = totals[query_owner[step], rows : rows + 1]
    for step in range(out.shape[0]):
        copy_out(totals, step).wait()


def last_scores(query_owner, left, before, units, names, scale):
    vmem, anywhere = pl.BlockSpec(memory_space=pltpu.VMEM), pl.BlockSpec(memory_space=pl.ANY)
    steps = query_owner.shape[0]
    _, rows, panel = before.shape
    return pl.pallas_call(
        functools.partial(last_kernel, names=names, scale=scale),
        in_specs=[pl.BlockSpec(memory_space=pltpu.SMEM)] + [vmem] * (2 + len(units)),
        out_specs=(anywhere, vmem),
        out_shape=(
            jax.ShapeDtypeStruct((steps, rows - 16, panel), jnp.float32),
            jax.ShapeDtypeStruct((steps, panel), jnp.float32),
        ),
        scratch_shapes=[pltpu.VMEM(before.shape, jnp.float32), pltpu.SemaphoreType.DMA((steps,))],
        compiler_params=pltpu.CompilerParams(vmem_limit_bytes=8 * MIB),
        cost_estimate=pl.CostEstimate(flops=1 << 30, bytes_accessed=8 * MIB, transcendentals=0),
    )(query_owner, left, before, *units)


def gate_kernel(block, *refs):
    del block, refs


def gate(block, *others):
    vmem, anywhere = pl.BlockSpec(memory_space=pltpu.VMEM), pl.BlockSpec(memory_space=pl.ANY)
    return pl.pallas_call(
        gate_kernel,
        in_specs=[anywhere] + [vmem if other.dtype == jnp.float32 else anywhere for other in others],
        out_specs=anywhere,
        out_shape=jax.ShapeDtypeStruct(block.shape, block.dtype),
        input_output_aliases={0: 0},
        compiler_params=pltpu.CompilerParams(vmem_limit_bytes=MIB),
        cost_estimate=pl.CostEstimate(flops=0, bytes_accessed=0, transcendentals=0),
    )(block, *others)


def plane_kernel(rows, sent, *refs):
    received, (kept, *sends) = refs[:3], refs[-4:]
    del sent
    store = lax.axis_index("store")
    z, x = store // 2, store % 2
    for place in range(rows.shape[0] // 2):
        kept[place] = rows[2 * place + x] + received[0][place] + received[1][place] + received[2][place]
    for bits, send in enumerate(sends):
        send[0] = kept[z ^ (bits + 1)]


def plane_moves(keep, send):
    return move(keep, "Y", "Y"), move(send, "X", "X"), move(send, "XY", "XY")


def sum_plane(rows, send, came, *tokens):
    vmem, anywhere = pl.BlockSpec(memory_space=pltpu.VMEM), pl.BlockSpec(memory_space=pl.ANY)
    count, tail = send.shape[0], send.shape[1:]
    return pl.pallas_call(
        plane_kernel,
        in_specs=[vmem] * 5 + [anywhere] * len(tokens),
        out_specs=[vmem] * 4,
        out_shape=[jax.ShapeDtypeStruct((count,) + tail, jnp.float32)]
        + [jax.ShapeDtypeStruct((1,) + tail, jnp.float32)] * 3,
        compiler_params=pltpu.CompilerParams(vmem_limit_bytes=4 * MIB),
        cost_estimate=pl.CostEstimate(flops=1 << 16, bytes_accessed=1 << 18, transcendentals=0),
    )(rows, send, *came, *tokens)


def line_kernel(rows, *refs):
    out = refs[-1]
    out[...] = rows[lax.axis_index("store") // 2] + refs[0][0] + refs[1][0] + refs[2][0]


def sum_line(rows, sends, *tokens):
    vmem, anywhere = pl.BlockSpec(memory_space=pltpu.VMEM), pl.BlockSpec(memory_space=pl.ANY)
    came = [move(send, way, way) for way, send in zip("STV", sends, strict=True)]
    return pl.pallas_call(
        line_kernel,
        in_specs=[vmem] * 4 + [anywhere] * len(tokens),
        out_specs=vmem,
        out_shape=jax.ShapeDtypeStruct(rows.shape[1:], jnp.float32),
        compiler_params=pltpu.CompilerParams(vmem_limit_bytes=4 * MIB),
        cost_estimate=pl.CostEstimate(flops=1 << 16, bytes_accessed=1 << 18, transcendentals=0),
    )(rows, *came, *tokens)


def split_kernel(rows, other, total, keep, send):
    x = lax.axis_index("store") % 2
    total[...] = rows[...] + other[...]
    for place in range(keep.shape[0]):
        keep[place] = total[2 * place + x]
        send[place] = total[2 * place + 1 - x]


def sum_cores(rows):
    vmem = pl.BlockSpec(memory_space=pltpu.VMEM)
    count, tail = rows.shape[0], rows.shape[1:]
    part = jax.ShapeDtypeStruct((count // 2,) + tail, jnp.float32)
    return pl.pallas_call(
        split_kernel,
        in_specs=[vmem] * 2,
        out_specs=[vmem] * 3,
        out_shape=[jax.ShapeDtypeStruct(rows.shape, jnp.float32), part, part],
        compiler_params=pltpu.CompilerParams(vmem_limit_bytes=4 * MIB),
        cost_estimate=pl.CostEstimate(flops=1 << 16, bytes_accessed=1 << 18, transcendentals=0),
    )(rows, move(rows, "C", "C", True))


def blocks(
    activations,
    out_grads,
    proj_in,
    proj_out,
    eig_out,
    eig_in,
    eig_values,
    lengths,
    owners,
    stored,
    queries,
    query_owner,
):
    seq = lax.axis_index("seq")
    seq_count, store_count = lax.axis_size("seq"), lax.axis_size("store")
    half = queries.shape[1] // 2
    got = {0: lax.dynamic_slice_in_dim(queries, ((seq // 2 + seq % 2) % 2) * half, half, 1)}
    partner = {}
    scale = 1.0 / math.sqrt(stored.shape[1])
    factor = 1.0 / math.sqrt(activations.shape[2] * seq_count)

    def step(number, part=None):
        source, way0, way1, swap = STEPS[number - 1]
        block = got[source]
        if part is None:
            got[number] = move(block, way0, way1, swap)
        else:
            width = half // 2
            got[number, part] = move(block[:, part * width : (part + 1) * width], way0, way1, swap)

    def swap(*numbers):
        for number in numbers:
            partner[number] = move(got[number], "C", "C", True)

    def pick(names):
        return [(partner if name[1] else got)[name[0]] for pair in names for name in pair if name is not None]

    def after(number, *others):
        got[number] = gate(got[number], *others)

    step(1)
    partial = project(
        activations[0], out_grads[0], proj_in[0], proj_out[0], lengths, owners, factor, store_count
    )
    after(1, partial)
    step(2)
    step(3, 0)
    swap(1)
    rows, keep, send = sum_cores(partial)
    rows, *sends = sum_plane(rows, send, plane_moves(keep, send), got[2])
    after(2, got[3, 0])
    step(4)
    step(3, 1)
    swap(2)
    row = sum_line(rows, sends, got[4])
    after(4, got[3, 1])
    step(5)
    step(6)
    swap(4)
    precond = precondition(row, eig_out[0], eig_in[0], eig_values[0]).reshape(1, -1)
    left, total, token = first_scores(stored, precond, queries, pick(EARLY), EARLY, scale, store_count)
    got[3] = jnp.concatenate([got[3, 0], got[3, 1]], axis=1)
    after(3, precond)
    step(7)
    after(5, token)
    swap(3, 5)
    total = next_scores(left, total, pick(THIRD), THIRD, scale)
    after(7, token)
    after(6, token)
    swap(6, 7)
    scores, group_out = last_scores(query_owner, left, total, pick(LAST), LAST, scale)
    return scores, group_out[None]


def from_root(array, axis, root):
    mine = lax.axis_index(axis) == root
    return lax.psum(jnp.where(mine, array, jnp.zeros_like(array)), axis)


def precondition_rows(group, eig_out, eig_in, eig_values):
    row_count = group.shape[0]
    layers = eig_out.shape[0]
    rank = eig_out.shape[1]
    split = group.reshape(row_count, layers, rank, rank)
    rotated = jnp.einsum("lri,olrs->olis", eig_out, split, precision=HIGHEST)
    rotated = jnp.einsum("olis,lsj->olij", rotated, eig_in, precision=HIGHEST)
    scaled = rotated / eig_values[None]
    restored = jnp.einsum("lri,olij->olrj", eig_out, scaled, precision=HIGHEST)
    restored = jnp.einsum("olrj,lsj->olrs", restored, eig_in, precision=HIGHEST)
    return restored.reshape(row_count, layers * rank * rank).astype(jnp.bfloat16)


def project_layer(inputs, outgoing, weight_in, weight_out, valid, factor):
    in_side = jnp.einsum("etd,rd->etr", inputs, weight_in, preferred_element_type=jnp.float32)
    out_side = jnp.einsum("etd,rd->etr", outgoing, weight_out, preferred_element_type=jnp.float32)
    weighted = out_side * valid[:, :, None]
    outer = jnp.einsum("etr,ets->ers", weighted, in_side, precision=HIGHEST) * factor
    return outer.reshape(outer.shape[0], -1)


def owner_sums(owners, sources, count):
    owner_ids = jnp.arange(count, dtype=jnp.int32)
    select = (owners[None, :] == owner_ids[:, None]).astype(jnp.float32)
    return jnp.dot(select, sources, precision=HIGHEST)


def any_mesh(
    activations,
    out_grads,
    proj_in,
    proj_out,
    eig_out,
    eig_in,
    eig_values,
    lengths,
    owners,
    stored,
    queries,
    query_owner,
):
    seq_count = lax.axis_size("seq")
    seq_index = lax.axis_index("seq")
    local_len = activations.shape[2]
    positions = seq_index * local_len + jnp.arange(local_len, dtype=jnp.int32)
    valid = (positions[None, :] < lengths[:, None]).astype(jnp.float32)
    factor = jnp.float32(1.0 / math.sqrt(local_len * seq_count))
    partial_value = project_layer(activations[0], out_grads[0], proj_in[0], proj_out[0], valid, factor)
    summed = lax.psum(partial_value, "seq")
    owned_row = lax.psum_scatter(
        owner_sums(owners, summed, lax.axis_size("store")), "store", scatter_dimension=0, tiled=True
    )
    precond = precondition_rows(owned_row, eig_out, eig_in, eig_values)
    score_scale = jnp.float32(1.0 / math.sqrt(stored.shape[1]))
    stored_list = []
    group_list = []
    for step_index in range(query_owner.shape[0]):
        panel_rows = from_root(queries, "store", query_owner[step_index])
        stored_list.append(
            lax.dot_general(stored, panel_rows, NT, preferred_element_type=jnp.float32) * score_scale
        )
        group_list.append(
            lax.dot_general(precond, panel_rows, NT, preferred_element_type=jnp.float32) * score_scale
        )
    return (jnp.stack(stored_list, axis=0), jnp.stack(group_list, axis=1))


def solution(mesh):
    fits = mesh.shape["store"] == 8 and mesh.shape["seq"] == 4
    return jax.shard_map(
        blocks if fits else any_mesh,
        mesh=mesh,
        in_specs=(
            P(None, "store", "seq", None),
            P(None, "store", "seq", None),
            P(),
            P(),
            P(),
            P(),
            P(),
            P("store"),
            P("store"),
            P(("store", "seq"), None),
            P("store", None),
            P(),
        ),
        out_specs=(P(None, ("store", "seq"), None), P("store", None, None)),
        check_vma=False,
    )
```

```python
import functools
import math

import jax
import jax.numpy as jnp
from jax import lax
from jax.experimental import pallas as pl
from jax.experimental.pallas import tpu as pltpu
from jax.sharding import PartitionSpec as P

AXES = ("store", "seq")
HIGHEST = lax.Precision.HIGHEST
NT = (((1,), (1,)), ((), ()))
MIB = 1 << 20

STEPS = (
    (0, "W", "X", True),
    (1, "Z", "X", False),
    (1, "Y", "Y", False),
    (2, "X", "W", False),
    (4, "Z", "X", False),
    (4, "Y", "Y", False),
    (3, "Z", "X", False),
)

FIRST = (((1, False), None), ((1, True), None))
SECOND = (((2, False), (4, False)), ((2, True), (4, True)))
THIRD = (((3, False), (5, True)), ((3, True), (5, False)))
LAST = (((6, False), (7, False)), ((6, True), (7, True)))


def ring_place(z):
    return z ^ (z >> 1)


def neighbour(way, z, x, y):
    if way == "X":
        return z, 1 - x, y
    if way == "Y":
        return z, x, 1 - y
    if way == "Z":
        return ring_place((ring_place(z) + 1) % 4), x, y
    if way == "W":
        return ring_place((ring_place(z) + 3) % 4), x, y
    if way == "S":
        return z ^ 1, x, y
    if way == "T":
        return z ^ 2, x, y
    if way == "V":
        return z ^ 3, x, y
    if way == "XY":
        return z, 1 - x, 1 - y
    return z, x, y
EARLY = FIRST + SECOND


def pairs(way0, way1, swap):
    out = []
    for z in range(4):
        for x in range(2):
            for y in range(2):
                for core in range(2):
                    z2, x2, y2 = neighbour(way1 if core else way0, z, x, y)
                    core2 = 1 - core if swap else core
                    out.append(((z * 2 + x) * 4 + y * 2 + core, (z2 * 2 + x2) * 4 + y2 * 2 + core2))
    return out


def move(array, way0, way1, swap=False):
    return lax.ppermute(array, AXES, pairs(way0, way1, swap))


def contents():
    have = [((0, 0, 0), (0, 0, 1))]
    for source, way0, way1, swap in STEPS:
        got = [None, None]
        for core, way in ((0, way0), (1, way1)):
            ring, across, half = have[source][core]
            if way == "X":
                across = 1 - across
            elif way == "Y":
                half = 1 - half
            elif way == "Z":
                ring = (ring + 1) % 4
            elif way == "W":
                ring = (ring + 3) % 4
            got[1 - core if swap else core] = (ring, across, half)
        have.append(tuple(got))
    return have


CONTENTS = contents()


def check_pairs():
    seen = [(0, 0, 0), (0, 0, 1)]
    for first, second in FIRST + SECOND + THIRD + LAST:
        for core in range(2):
            one = CONTENTS[first[0]][core ^ first[1]]
            seen.append(one)
            if second is not None:
                two = CONTENTS[second[0]][core ^ second[1]]
                seen.append(two)
                assert one[2] == two[2]
    assert len(set(seen)) == 16


check_pairs()


def unit_place(step, partner, store, seq):
    y, core = seq // 2, seq % 2
    z, x = store // 2, store % 2
    first, second = CONTENTS[step]
    mine = core if not partner else 1 - core
    pick = [jnp.where(mine == 0, a, b) for a, b in zip(first, second, strict=True)]
    place = (ring_place(z) + 4 - pick[0]) % 4
    return ring_place(place) * 2 + (x ^ pick[1]), pick[2] ^ y


def outer_kernel(lengths, owners, in_side, out_side, out, *, factor):
    examples, _, tokens = in_side.shape
    start = lax.axis_index("seq") * tokens
    sums = []
    for e in range(examples):
        outgoing = out_side[e]
        positions = start + lax.broadcasted_iota(jnp.int32, outgoing.shape, 1)
        outgoing = jnp.where(positions < lengths[e], outgoing, 0.0)
        block = lax.dot_general(outgoing, in_side[e], NT, precision=HIGHEST, preferred_element_type=jnp.float32)
        half = block.shape[0] // 2
        sums.append(jnp.concatenate([block[:half], block[half:]], axis=1) * factor)
    for owner in range(out.shape[0]):
        acc = jnp.zeros_like(sums[0])
        for e in range(examples):
            acc += jnp.where(owners[e] == owner, sums[e], 0.0)
        out[owner] = acc


def project(acts, grads, weight_in, weight_out, lengths, owners, factor, owner_count):
    in_side = jnp.einsum("rd,etd->ert", weight_in, acts, preferred_element_type=jnp.float32)
    out_side = jnp.einsum("rd,etd->ert", weight_out, grads, preferred_element_type=jnp.float32)
    rank = weight_in.shape[0]
    smem, vmem = pl.BlockSpec(memory_space=pltpu.SMEM), pl.BlockSpec(memory_space=pltpu.VMEM)
    return pl.pallas_call(
        functools.partial(outer_kernel, factor=factor),
        in_specs=[smem, smem, vmem, vmem],
        out_specs=vmem,
        out_shape=jax.ShapeDtypeStruct((owner_count, rank // 2, rank * 2), jnp.float32),
        compiler_params=pltpu.CompilerParams(vmem_limit_bytes=4 * MIB),
        cost_estimate=pl.CostEstimate(flops=1 << 26, bytes_accessed=1 << 19, transcendentals=0),
    )(lengths, owners, in_side, out_side)


def precondition_kernel(group, eig_out, eig_in, eig_values, out):
    rank = eig_out.shape[0]
    packed = group[...]
    block = jnp.concatenate([packed[:, :rank], packed[:, rank:]], axis=0)
    dot = functools.partial(lax.dot_general, precision=HIGHEST, preferred_element_type=jnp.float32)
    basis_out, basis_in = eig_out[...], eig_in[...]
    rotated = dot(basis_out, block, (((0,), (0,)), ((), ())))
    rotated = dot(rotated, basis_in, (((1,), (0,)), ((), ())))
    scaled = rotated / eig_values[...]
    restored = dot(basis_out, scaled, (((1,), (0,)), ((), ())))
    restored = dot(restored, basis_in, NT)
    out[...] = restored.astype(jnp.bfloat16)


def precondition(group, eig_out, eig_in, eig_values):
    rank = eig_out.shape[0]
    return pl.pallas_call(
        precondition_kernel,
        out_shape=jax.ShapeDtypeStruct((rank, rank), jnp.bfloat16),
        compiler_params=pltpu.CompilerParams(vmem_limit_bytes=4 * MIB),
        cost_estimate=pl.CostEstimate(flops=1 << 24, bytes_accessed=1 << 17, transcendentals=0),
    )(group, eig_out, eig_in, eig_values)


def add_scores(left, own, blocks, names, totals, scale):
    store, seq = lax.axis_index("store"), lax.axis_index("seq")
    for first, second in names:
        panel, half = unit_place(*first, store, seq)
        block = next(blocks)
        rows, width = block.shape
        columns = pl.ds(pl.multiple_of(half * width, width), width)
        if second is None:
            other_panel, other = store, own[:, columns]
        else:
            other_panel, other = unit_place(*second, store, seq)[0], next(blocks)
        product = lax.dot_general(
            left[:, columns], jnp.concatenate([block, other], axis=0), NT, preferred_element_type=jnp.float32
        )
        totals[panel] += product[:, :rows] * scale
        totals[other_panel] += product[:, rows:] * scale


def brought(units, buffer, sems):
    copies = [pltpu.make_async_copy(unit, buffer.at[n], sems.at[n]) for n, unit in enumerate(units)]
    for copy in copies:
        copy.start()

    def each():
        for n, copy in enumerate(copies):
            copy.wait()
            yield buffer[n]

    return each()


def first_kernel(stored, row, own, *refs, names, scale):
    units, (left, totals, token, buffer, sems, own_buffer, own_sems) = refs[:-7], refs[-7:]
    rows = stored.shape[0]
    copies = (
        pltpu.make_async_copy(stored, left.at[pl.ds(0, rows)], own_sems.at[0]),
        pltpu.make_async_copy(own, own_buffer, own_sems.at[1]),
    )
    for copy in copies:
        copy.start()
    blocks = brought(units, buffer, sems)
    token[...] = jnp.zeros_like(token)
    left[rows:] = jnp.broadcast_to(row[...], (left.shape[0] - rows, row.shape[1]))
    totals[...] = jnp.zeros_like(totals)
    for copy in copies:
        copy.wait()
    add_scores(left, own_buffer, blocks, names, totals, scale)


def first_scores(stored, row, own, units, names, scale, panels):
    vmem, anywhere = pl.BlockSpec(memory_space=pltpu.VMEM), pl.BlockSpec(memory_space=pl.ANY)
    rows, width = stored.shape
    panel = own.shape[0]
    return pl.pallas_call(
        functools.partial(first_kernel, names=names, scale=scale),
        in_specs=[anywhere, vmem, anywhere] + [anywhere] * len(units),
        out_specs=(vmem, vmem, vmem),
        out_shape=(
            jax.ShapeDtypeStruct((rows + 16, width), jnp.bfloat16),
            jax.ShapeDtypeStruct((panels, rows + 16, panel), jnp.float32),
            jax.ShapeDtypeStruct((8, 128), jnp.float32),
        ),
        scratch_shapes=[
            pltpu.VMEM((len(units),) + units[0].shape, jnp.bfloat16),
            pltpu.SemaphoreType.DMA((len(units),)),
            pltpu.VMEM(own.shape, jnp.bfloat16),
            pltpu.SemaphoreType.DMA((2,)),
        ],
        compiler_params=pltpu.CompilerParams(vmem_limit_bytes=20 * MIB),
        cost_estimate=pl.CostEstimate(flops=1 << 33, bytes_accessed=1024, transcendentals=0),
    )(stored, row, own, *units)


def next_kernel(left, before, *refs, names, scale):
    units, (totals, buffer, sems) = refs[:-3], refs[-3:]
    blocks = brought(units, buffer, sems)
    totals[...] = before[...]
    add_scores(left, None, blocks, names, totals, scale)


def next_scores(left, before, units, names, scale):
    vmem, anywhere = pl.BlockSpec(memory_space=pltpu.VMEM), pl.BlockSpec(memory_space=pl.ANY)
    return pl.pallas_call(
        functools.partial(next_kernel, names=names, scale=scale),
        in_specs=[vmem, vmem] + [anywhere] * len(units),
        out_specs=vmem,
        out_shape=jax.ShapeDtypeStruct(before.shape, jnp.float32),
        scratch_shapes=[
            pltpu.VMEM((len(units),) + units[0].shape, jnp.bfloat16),
            pltpu.SemaphoreType.DMA((len(units),)),
        ],
        compiler_params=pltpu.CompilerParams(vmem_limit_bytes=8 * MIB),
        cost_estimate=pl.CostEstimate(flops=1 << 32, bytes_accessed=1024, transcendentals=0),
    )(left, before, *units)


def last_kernel(query_owner, left, before, *refs, names, scale):
    units, (out, group_out, totals, sems) = refs[:-4], refs[-4:]
    rows = out.shape[1]
    store, seq = lax.axis_index("store"), lax.axis_index("seq")
    late = [unit_place(*name, store, seq)[0] for pair in names for name in pair]

    def copy_out(source, step):
        return pltpu.make_async_copy(source.at[query_owner[step], pl.ds(0, rows)], out.at[step], sems.at[step])

    def is_late(step):
        found = query_owner[step] == late[0]
        for panel in late[1:]:
            found = found | (query_owner[step] == panel)
        return found

    for step in range(out.shape[0]):

        @pl.when(jnp.logical_not(is_late(step)))
        def _(step=step):
            copy_out(before, step).start()

    for panel in late:
        totals[panel] = before[panel]
    add_scores(left, None, iter([unit[...] for unit in units]), names, totals, scale)
    for step in range(out.shape[0]):

        @pl.when(is_late(step))
        def _(step=step):
            copy_out(totals, step).start()
            group_out[pl.ds(step, 1)] = totals[query_owner[step], rows : rows + 1]

        @pl.when(jnp.logical_not(is_late(step)))
        def _(step=step):
            group_out[pl.ds(step, 1)] = before[query_owner[step], rows : rows + 1]
    for step in range(out.shape[0]):
        copy_out(totals, step).wait()


def last_scores(query_owner, left, before, units, names, scale):
    vmem, anywhere = pl.BlockSpec(memory_space=pltpu.VMEM), pl.BlockSpec(memory_space=pl.ANY)
    steps = query_owner.shape[0]
    _, rows, panel = before.shape
    return pl.pallas_call(
        functools.partial(last_kernel, names=names, scale=scale),
        in_specs=[pl.BlockSpec(memory_space=pltpu.SMEM)] + [vmem] * (2 + len(units)),
        out_specs=(anywhere, vmem),
        out_shape=(
            jax.ShapeDtypeStruct((steps, rows - 16, panel), jnp.float32),
            jax.ShapeDtypeStruct((steps, panel), jnp.float32),
        ),
        scratch_shapes=[pltpu.VMEM(before.shape, jnp.float32), pltpu.SemaphoreType.DMA((steps,))],
        compiler_params=pltpu.CompilerParams(vmem_limit_bytes=8 * MIB),
        cost_estimate=pl.CostEstimate(flops=1 << 30, bytes_accessed=8 * MIB, transcendentals=0),
    )(query_owner, left, before, *units)


def gate_kernel(block, *refs):
    del block, refs


def gate(block, *others):
    vmem, anywhere = pl.BlockSpec(memory_space=pltpu.VMEM), pl.BlockSpec(memory_space=pl.ANY)
    return pl.pallas_call(
        gate_kernel,
        in_specs=[anywhere] + [vmem if other.dtype == jnp.float32 else anywhere for other in others],
        out_specs=anywhere,
        out_shape=jax.ShapeDtypeStruct(block.shape, block.dtype),
        input_output_aliases={0: 0},
        compiler_params=pltpu.CompilerParams(vmem_limit_bytes=MIB),
        cost_estimate=pl.CostEstimate(flops=0, bytes_accessed=0, transcendentals=0),
    )(block, *others)


def plane_kernel(rows, sent, *refs):
    received, (kept, *sends) = refs[:3], refs[-4:]
    del sent
    store = lax.axis_index("store")
    z, x = store // 2, store % 2
    for place in range(rows.shape[0] // 2):
        kept[place] = rows[2 * place + x] + received[0][place] + received[1][place] + received[2][place]
    for bits, send in enumerate(sends):
        send[0] = kept[z ^ (bits + 1)]


def plane_moves(keep, send):
    return move(keep, "Y", "Y"), move(send, "X", "X"), move(send, "XY", "XY")


def sum_plane(rows, send, came, *tokens):
    vmem, anywhere = pl.BlockSpec(memory_space=pltpu.VMEM), pl.BlockSpec(memory_space=pl.ANY)
    count, tail = send.shape[0], send.shape[1:]
    return pl.pallas_call(
        plane_kernel,
        in_specs=[vmem] * 5 + [anywhere] * len(tokens),
        out_specs=[vmem] * 4,
        out_shape=[jax.ShapeDtypeStruct((count,) + tail, jnp.float32)]
        + [jax.ShapeDtypeStruct((1,) + tail, jnp.float32)] * 3,
        compiler_params=pltpu.CompilerParams(vmem_limit_bytes=4 * MIB),
        cost_estimate=pl.CostEstimate(flops=1 << 28, bytes_accessed=1 << 18, transcendentals=0),
    )(rows, send, *came, *tokens)


def line_kernel(rows, *refs):
    out = refs[-1]
    out[...] = rows[lax.axis_index("store") // 2] + refs[0][0] + refs[1][0] + refs[2][0]


def sum_line(rows, sends, *tokens):
    vmem, anywhere = pl.BlockSpec(memory_space=pltpu.VMEM), pl.BlockSpec(memory_space=pl.ANY)
    came = [move(send, way, way) for way, send in zip("STV", sends, strict=True)]
    return pl.pallas_call(
        line_kernel,
        in_specs=[vmem] * 4 + [anywhere] * len(tokens),
        out_specs=vmem,
        out_shape=jax.ShapeDtypeStruct(rows.shape[1:], jnp.float32),
        compiler_params=pltpu.CompilerParams(vmem_limit_bytes=4 * MIB),
        cost_estimate=pl.CostEstimate(flops=1 << 28, bytes_accessed=1 << 18, transcendentals=0),
    )(rows, *came, *tokens)


def split_kernel(rows, other, total, keep, send):
    x = lax.axis_index("store") % 2
    total[...] = rows[...] + other[...]
    for place in range(keep.shape[0]):
        keep[place] = total[2 * place + x]
        send[place] = total[2 * place + 1 - x]


def sum_cores(rows):
    vmem = pl.BlockSpec(memory_space=pltpu.VMEM)
    count, tail = rows.shape[0], rows.shape[1:]
    part = jax.ShapeDtypeStruct((count // 2,) + tail, jnp.float32)
    return pl.pallas_call(
        split_kernel,
        in_specs=[vmem] * 2,
        out_specs=[vmem] * 3,
        out_shape=[jax.ShapeDtypeStruct(rows.shape, jnp.float32), part, part],
        compiler_params=pltpu.CompilerParams(vmem_limit_bytes=4 * MIB),
        cost_estimate=pl.CostEstimate(flops=1 << 16, bytes_accessed=1 << 18, transcendentals=0),
    )(rows, move(rows, "C", "C", True))


def blocks(
    activations,
    out_grads,
    proj_in,
    proj_out,
    eig_out,
    eig_in,
    eig_values,
    lengths,
    owners,
    stored,
    queries,
    query_owner,
):
    seq = lax.axis_index("seq")
    seq_count, store_count = lax.axis_size("seq"), lax.axis_size("store")
    half = queries.shape[1] // 2
    got = {0: lax.dynamic_slice_in_dim(queries, ((seq // 2 + seq % 2) % 2) * half, half, 1)}
    partner = {}
    scale = 1.0 / math.sqrt(stored.shape[1])
    factor = 1.0 / math.sqrt(activations.shape[2] * seq_count)

    def step(number, part=None):
        source, way0, way1, swap = STEPS[number - 1]
        block = got[source]
        if part is None:
            got[number] = move(block, way0, way1, swap)
        else:
            width = half // 2
            got[number, part] = move(block[:, part * width : (part + 1) * width], way0, way1, swap)

    def swap(*numbers):
        for number in numbers:
            partner[number] = move(got[number], "C", "C", True)

    def pick(names):
        return [(partner if name[1] else got)[name[0]] for pair in names for name in pair if name is not None]

    def after(number, *others):
        got[number] = gate(got[number], *others)

    step(1)
    partial = project(
        activations[0], out_grads[0], proj_in[0], proj_out[0], lengths, owners, factor, store_count
    )
    after(1, partial)
    step(2)
    step(3, 0)
    swap(1)
    rows, keep, send = sum_cores(partial)
    rows, *sends = sum_plane(rows, send, plane_moves(keep, send), got[2])
    after(2, got[3, 0])
    step(4)
    step(3, 1)
    swap(2)
    row = sum_line(rows, sends, got[4])
    after(4, got[3, 1])
    step(5)
    step(6)
    swap(4)
    precond = precondition(row, eig_out[0], eig_in[0], eig_values[0]).reshape(1, -1)
    left, total, token = first_scores(stored, precond, queries, pick(EARLY), EARLY, scale, store_count)
    got[3] = jnp.concatenate([got[3, 0], got[3, 1]], axis=1)
    after(3, precond)
    step(7)
    after(5, token)
    swap(3, 5)
    total = next_scores(left, total, pick(THIRD), THIRD, scale)
    after(7, token)
    after(6, token)
    swap(6, 7)
    scores, group_out = last_scores(query_owner, left, total, pick(LAST), LAST, scale)
    return scores, group_out[None]


def from_root(array, axis, root):
    mine = lax.axis_index(axis) == root
    return lax.psum(jnp.where(mine, array, jnp.zeros_like(array)), axis)


def precondition_rows(group, eig_out, eig_in, eig_values):
    row_count = group.shape[0]
    layers = eig_out.shape[0]
    rank = eig_out.shape[1]
    split = group.reshape(row_count, layers, rank, rank)
    rotated = jnp.einsum("lri,olrs->olis", eig_out, split, precision=HIGHEST)
    rotated = jnp.einsum("olis,lsj->olij", rotated, eig_in, precision=HIGHEST)
    scaled = rotated / eig_values[None]
    restored = jnp.einsum("lri,olij->olrj", eig_out, scaled, precision=HIGHEST)
    restored = jnp.einsum("olrj,lsj->olrs", restored, eig_in, precision=HIGHEST)
    return restored.reshape(row_count, layers * rank * rank).astype(jnp.bfloat16)


def project_layer(inputs, outgoing, weight_in, weight_out, valid, factor):
    in_side = jnp.einsum("etd,rd->etr", inputs, weight_in, preferred_element_type=jnp.float32)
    out_side = jnp.einsum("etd,rd->etr", outgoing, weight_out, preferred_element_type=jnp.float32)
    weighted = out_side * valid[:, :, None]
    outer = jnp.einsum("etr,ets->ers", weighted, in_side, precision=HIGHEST) * factor
    return outer.reshape(outer.shape[0], -1)


def owner_sums(owners, sources, count):
    owner_ids = jnp.arange(count, dtype=jnp.int32)
    select = (owners[None, :] == owner_ids[:, None]).astype(jnp.float32)
    return jnp.dot(select, sources, precision=HIGHEST)


def any_mesh(
    activations,
    out_grads,
    proj_in,
    proj_out,
    eig_out,
    eig_in,
    eig_values,
    lengths,
    owners,
    stored,
    queries,
    query_owner,
):
    seq_count = lax.axis_size("seq")
    seq_index = lax.axis_index("seq")
    local_len = activations.shape[2]
    positions = seq_index * local_len + jnp.arange(local_len, dtype=jnp.int32)
    valid = (positions[None, :] < lengths[:, None]).astype(jnp.float32)
    factor = jnp.float32(1.0 / math.sqrt(local_len * seq_count))
    partial_value = project_layer(activations[0], out_grads[0], proj_in[0], proj_out[0], valid, factor)
    summed = lax.psum(partial_value, "seq")
    owned_row = lax.psum_scatter(
        owner_sums(owners, summed, lax.axis_size("store")), "store", scatter_dimension=0, tiled=True
    )
    precond = precondition_rows(owned_row, eig_out, eig_in, eig_values)
    score_scale = jnp.float32(1.0 / math.sqrt(stored.shape[1]))
    stored_list = []
    group_list = []
    for step_index in range(query_owner.shape[0]):
        panel_rows = from_root(queries, "store", query_owner[step_index])
        stored_list.append(
            lax.dot_general(stored, panel_rows, NT, preferred_element_type=jnp.float32) * score_scale
        )
        group_list.append(
            lax.dot_general(precond, panel_rows, NT, preferred_element_type=jnp.float32) * score_scale
        )
    return (jnp.stack(stored_list, axis=0), jnp.stack(group_list, axis=1))


def solution(mesh):
    fits = mesh.shape["store"] == 8 and mesh.shape["seq"] == 4
    return jax.shard_map(
        blocks if fits else any_mesh,
        mesh=mesh,
        in_specs=(
            P(None, "store", "seq", None),
            P(None, "store", "seq", None),
            P(),
            P(),
            P(),
            P(),
            P(),
            P("store"),
            P("store"),
            P(("store", "seq"), None),
            P("store", None),
            P(),
        ),
        out_specs=(P(None, ("store", "seq"), None), P("store", None, None)),
        check_vma=False,
    )
```
